128 devices in a mesh: patch: 32 (over x, y, z_lo), head: 4 (over z_hi, core).
Axes of the slice: x: 4, y: 4, z: 4 (z_hi: 2, z_lo: 2; z = z_hi * 2 + z_lo), core: 2. Of those that a mesh axis runs over, the one named last changes fastest.
Arguments:
- feature: bfloat16 [128, 96, 1280], P('patch', None, 'head'), may hold values from -6 to 6
- prev_feature: bfloat16 [128, 96, 1280], P('patch', None, 'head'), may hold values from -60 to 60, as said below
- conv_weight: bfloat16 [3, 3, 1280, 1280], P(None, None, None, 'head'), may hold values from -0.0546875 to 0.0546875
- w_query: bfloat16 [1280, 1280], P(None, 'head'), may hold values from -0.15625 to 0.15625
- w_key: bfloat16 [1280, 1280], P(None, 'head'), may hold values from -0.5 to 0.5
- w_value: bfloat16 [1280, 1280], P(None, 'head'), may hold values from -0.3125 to 0.3125
- w_out: bfloat16 [1280, 1280], P('head'), may hold values from -0.15625 to 0.15625
- prev_keys: bfloat16 [12288, 1280], P('patch', 'head'), may hold values from -300 to 300
- prev_values: bfloat16 [12288, 1280], P('patch', 'head'), may hold values from -8 to 8
Outputs:
- resnet_out: float32 [128, 96, 1280], P('patch', None, 'head')
- attended: float32 [12288, 1280], P('patch', 'head')
The draws below stay inside these ranges and needn't reach their ends.
Inputs may be any that keep to these rules, and one draw needn't show every extreme that they name: `prev_feature`: the previous step's feature map.
All inputs are finite; a program needn't handle non-finite values.
Results may differ from the reference program's by a relative error of at most 0.035.
Values may be sent and summed in bfloat16 or wider, within the bound.
A program may use at most 128 MiB of HBM per device.

```python
import jax
import jax.numpy as jnp
from jax import lax

C = 1280
HEADS = 20
GROUPS = 32
HEAD_DIM = 64
ROWS_DEV = 4
COLS = 96
IMG_ROWS = 128
TOK_DEV = 384
TOKENS = 12288
N_PATCH = 32


def draw_prev_feature(key, part):
    key = jax.random.fold_in(key, 11)
    first, second, third = jax.random.split(key, 3)
    height = jnp.arange(IMG_ROWS, dtype=jnp.float32) / max(IMG_ROWS - 1, 1)
    base = jax.random.normal(first, (IMG_ROWS, COLS, C), jnp.float32)
    rise = jnp.log(3.0)
    rough = jnp.exp(jax.random.uniform(second, (IMG_ROWS, 1, 1), jnp.float32, -0.15, 0.15))
    scale = jnp.exp(rise * height)[:, None, None] * rough
    centre = jax.random.uniform(third, (1, 1, C), jnp.float32, -1.0, 1.0)
    return jnp.clip((centre + base) * scale, -60.0, 60.0).astype(jnp.bfloat16)


def draw_prev_keys(key, part):
    key = jax.random.fold_in(key, 12)
    first, second = jax.random.split(key, 2)
    blocks = TOKENS // TOK_DEV
    offset = jax.random.normal(second, (blocks, 1, C), jnp.float32) * 0.7
    offset = jnp.broadcast_to(offset, (blocks, TOK_DEV, C)).reshape(TOKENS, C)
    base = jax.random.normal(first, (TOKENS, C), jnp.float32) * 3.0
    return jnp.clip(base + offset, -300.0, 300.0).astype(jnp.bfloat16)


def draw_prev_values(key, part):
    key = jax.random.fold_in(key, 13)
    first, second = jax.random.split(key, 2)
    blocks = TOKENS // TOK_DEV
    offset = jax.random.normal(second, (blocks, 1, C), jnp.float32)
    offset = jnp.broadcast_to(offset, (blocks, TOK_DEV, C)).reshape(TOKENS, C)
    base = jax.random.normal(first, (TOKENS, C), jnp.float32) * 2.0
    return jnp.clip(base + offset, -8.0, 8.0).astype(jnp.bfloat16)


def shard_levels(own_key, extent, pieces, smallest, top_value):
    factor_of = 1.0
    for axis_at, shards_of in pieces:
        steps = jax.random.uniform(jax.random.fold_in(jax.random.fold_in(own_key, 6), axis_at), (shards_of,), jnp.float32, smallest / len(pieces), top_value / len(pieces))
        factor_of = factor_of * jnp.repeat(jnp.exp(steps), extent[axis_at] // shards_of).reshape((-1,) + (1,) * (len(extent) - 1 - axis_at))
    return factor_of


def scatter_about(stream_key, shape, scale, limit, cuts=(), held_as=jnp.bfloat16):
    level = shard_levels(stream_key, shape, cuts, -0.22, 0.18) if cuts else 1.0
    entries = jax.random.normal(stream_key, shape, jnp.float32) * scale * level
    return jnp.minimum(jnp.maximum(entries, -limit), limit).astype(held_as)


def setup_inputs(seed: int = 0) -> dict:
    key_list = jax.random.split(jax.random.key(seed), 10)
    return {
        "feature": scatter_about(key_list[0], (IMG_ROWS, COLS, C), 1.0, 6.0, ((0, 32), (2, 4))),
        "prev_feature": draw_prev_feature(jax.random.fold_in(key_list[9], 71), 0),
        "conv_weight": scatter_about(key_list[2], (3, 3, C, C), (9 * C) ** -0.5, 0.0546875, ((3, 4),)),
        "w_query": scatter_about(key_list[3], (C, C), C ** -0.5, 0.15625, ((1, 4),)),
        "w_key": scatter_about(key_list[4], (C, C), (C // 9) ** -0.5, 0.5, ((1, 4),)),
        "w_value": scatter_about(key_list[5], (C, C), (C // 4) ** -0.5, 0.3125, ((1, 4),)),
        "w_out": scatter_about(key_list[6], (C, C), C ** -0.5, 0.15625, ((0, 4),)),
        "prev_keys": draw_prev_keys(jax.random.fold_in(key_list[9], 71), 0),
        "prev_values": draw_prev_values(jax.random.fold_in(key_list[9], 71), 0),
    }


def activate(values, centre, rstd):
    grouped = values.astype(jnp.float32).reshape(values.shape[0], values.shape[1], GROUPS, -1)
    scaled = (grouped - centre[:, None]) * rstd[:, None]
    return jax.nn.silu(scaled).reshape(values.shape).astype(jnp.bfloat16)

def reference(feature, prev_feature, conv_weight, w_query, w_key, w_value, w_out, prev_keys, prev_values):
    group_width = C // GROUPS
    stale_in = prev_feature.astype(jnp.float32).reshape(IMG_ROWS * COLS, GROUPS, group_width)
    count = IMG_ROWS * COLS * group_width
    centre = lax.optimization_barrier(jnp.sum(stale_in, axis=(0, 2))) / count
    spread = lax.optimization_barrier(jnp.sum(stale_in * stale_in, axis=(0, 2))) / count - centre * centre
    rstd = lax.rsqrt(spread + 1e-05)
    fresh = activate(feature, centre, rstd)
    stale = activate(prev_feature, centre, rstd)
    zero_row = jnp.zeros((1, COLS, C), jnp.bfloat16)
    row_ids = jnp.arange(IMG_ROWS, dtype=jnp.int32)
    is_top = (row_ids % ROWS_DEV == 0)[:, None, None]
    is_bottom = ((row_ids + 1) % ROWS_DEV == 0)[:, None, None]
    above = jnp.where(is_top, jnp.concatenate([zero_row, stale[:-1]], 0), jnp.concatenate([zero_row, fresh[:-1]], 0))
    below = jnp.where(is_bottom, jnp.concatenate([stale[1:], zero_row], 0), jnp.concatenate([fresh[1:], zero_row], 0))
    conv = jnp.zeros((IMG_ROWS * COLS, C), jnp.float32)
    for offset_y, source in enumerate([above, fresh, below]):
        wide = jnp.pad(source, ((0, 0), (1, 1), (0, 0)))
        for offset_x in range(3):
            window = wide[:, offset_x:offset_x + COLS].reshape(IMG_ROWS * COLS, C)
            conv = conv + jnp.dot(window, conv_weight[offset_y, offset_x], preferred_element_type=jnp.float32)
    resnet_out = feature.astype(jnp.float32).reshape(IMG_ROWS * COLS, C) + conv
    flat = resnet_out
    mean_tok = lax.optimization_barrier(jnp.mean(flat, axis=1, keepdims=True))
    var_tok = lax.optimization_barrier(jnp.mean(flat * flat, axis=1, keepdims=True)) - mean_tok * mean_tok
    normed = ((flat - mean_tok) * lax.rsqrt(var_tok + 1e-05)).astype(jnp.bfloat16)
    query = jnp.dot(normed, w_query, preferred_element_type=jnp.float32).astype(jnp.bfloat16)
    key = jnp.dot(normed, w_key, preferred_element_type=jnp.float32).astype(jnp.bfloat16)
    value = jnp.dot(normed, w_value, preferred_element_type=jnp.float32).astype(jnp.bfloat16)
    scale = 1.0 / HEAD_DIM ** 0.5

    def one_block(block):
        first = (block * TOK_DEV).astype(jnp.int32)
        block_q = lax.dynamic_slice_in_dim(query, first, TOK_DEV, 0)
        keys_b = lax.dynamic_update_slice_in_dim(prev_keys, lax.dynamic_slice_in_dim(key, first, TOK_DEV, 0), first, 0)
        values_b = lax.dynamic_update_slice_in_dim(prev_values, lax.dynamic_slice_in_dim(value, first, TOK_DEV, 0), first, 0)
        q3 = block_q.astype(jnp.float32).reshape(TOK_DEV, HEADS, HEAD_DIM)
        k3 = keys_b.astype(jnp.float32).reshape(TOKENS, HEADS, HEAD_DIM)
        v3 = values_b.astype(jnp.float32).reshape(TOKENS, HEADS, HEAD_DIM)
        scores = jnp.einsum('qhd,khd->hqk', q3, k3) * scale
        top = lax.optimization_barrier(jnp.max(scores, axis=-1, keepdims=True))
        expo = jnp.exp(scores - top)
        total = lax.optimization_barrier(jnp.sum(expo, axis=-1))
        weights = expo.astype(jnp.bfloat16).astype(jnp.float32)
        summed = jnp.einsum('hqk,khd->hqd', weights, v3)
        heads_out = summed / total[..., None]
        return heads_out.transpose(1, 0, 2).reshape(TOK_DEV, C).astype(jnp.bfloat16)
    heads_all = lax.map(one_block, jnp.arange(N_PATCH, dtype=jnp.int32)).reshape(TOKENS, C)
    attended = jnp.dot(heads_all, w_out, preferred_element_type=jnp.float32)
    return (resnet_out.reshape(IMG_ROWS, COLS, C), attended)
```

```python
import functools

import jax
import jax.numpy as jnp
from jax import lax
from jax.experimental import pallas as pl
from jax.experimental.pallas import tpu as pltpu
from jax.sharding import PartitionSpec as P

C = 1280
GROUPS = 32
HEAD_DIM = 64
TOK = 384
COLS = 96
WIDTH = 320
HEADS_DEV = 5
CHUNK = 4 * TOK
FIRST_OWN = 0
FIRST_OTHER = TOK
SECOND = 5 * TOK
PLACE = {0: 4, 1: 1, 2: 2, 3: 3, 4: 5, 5: 6, 6: 7, 7: 8}
NT = (((1,), (1,)), ((), ()))
N_PATCH = 32
COUNT = 128 * 96 * (C // GROUPS)
SCORE_SCALE = 1.4426950408889634 / HEAD_DIM**0.5
BF16 = jnp.bfloat16
F32 = jnp.float32
MESH = pl.DeviceIdType.MESH

SEM_FEATURE = 0
SEM_ROWS = 6
SEM_RIMS = 10
SEM_TOKENS = 12
SEM_W_OUT = 24
SEM_STATS_HEAD = 27
SEM_STATS_KEY = 30
SEM_STATS_QUERY = 37
SEM_QUERY = 40
SEM_KEY = 43
SEM_VALUE = 51
SEM_PARTIAL = 59
SEM_LEVEL = 74
SEM_HEADS = 89
SEMS = 109


def kernel(
    feature,
    prev_feature,
    conv_weight,
    w_query,
    w_key,
    w_value,
    w_out,
    prev_keys,
    prev_values,
    resnet_ref,
    attended_ref,
    raw,
    prev_in,
    sums_own,
    sums_key,
    sums_query,
    sums_head,
    groups,
    slopes,
    act,
    conv_w,
    qkv_w,
    conv_part,
    res_out,
    tokens,
    normed,
    queries,
    query_heads,
    key_t,
    value_t,
    scores,
    tops,
    part,
    partial_out,
    partial_in,
    level_out,
    level_in,
    relay_feature,
    relay_tokens,
    relay_heads,
    heads,
    out_w,
    out_w_send,
    out_w_rows,
    attended,
    send,
    recv,
    local,
):
    p = lax.axis_index("patch")
    h = lax.axis_index("head")
    x, y, zl = p // 8, (p // 2) % 4, p % 2

    def at(xx, yy, zz):
        return xx * 8 + yy * 2 + zz

    xn = x + 1 - 2 * (x % 2)
    xf = (x + 2) % 4
    y1, y2, y3 = (y + 1) % 4, (y + 2) % 4, (y + 3) % 4
    zh, core = h // 2, h % 2
    h_chip = zh * 2 + 1 - core
    h_far = (1 - zh) * 2 + core
    h_diag = (1 - zh) * 2 + 1 - core
    h_up = ((zh + zl) % 2) * 2 + core
    h_down = ((zh + 1 - zl) % 2) * 2 + core

    dev_chip, dev_far, dev_diag = (p, h_chip), (p, h_far), (p, h_diag)
    dev_up, dev_down = (at(x, y, 1 - zl), h_up), (at(x, y, 1 - zl), h_down)
    key_peers = [
        (at(x, y1, zl), h),
        (at(x, y3, zl), h),
        (at(x, y2, zl), h),
        (at(xf, y, zl), h),
        (at(xf, y1, zl), h),
        (at(xf, y3, zl), h),
        (at(xf, y2, zl), h),
    ]
    dev_y1, dev_y3, dev_y2, dev_xf = key_peers[:4]
    query_peers = [(at(x, y, 1 - zl), h), (at(xn, y, zl), h), (at(xn, y, 1 - zl), h)]
    p_next, p_prev = (p + 1) % N_PATCH, (p + N_PATCH - 1) % N_PATCH
    rim_peers = [(p_next, h), (p_next, h_far), (p_prev, h), (p_prev, h_far)]

    started = []

    def copy(src, dst, sem_send, sem_recv, device):
        return pltpu.make_async_remote_copy(
            src_ref=src,
            dst_ref=dst,
            send_sem=send.at[sem_send],
            recv_sem=recv.at[sem_recv],
            device_id=device,
            device_id_type=MESH,
        )

    def push(src, dst, sem, device, sem_send=None):
        c = copy(src, dst, sem if sem_send is None else sem_send, sem, device)
        c.start()
        started.append(c)

    def arrived(dst, sem, device):
        copy(dst, dst, sem, sem, device).wait_recv()

    def fetch(src, dst, sem):
        c = pltpu.make_async_copy(src, dst, local.at[sem])
        c.start()
        return c

    def columns(slot):
        return slice(PLACE[slot] * TOK, (PLACE[slot] + 1) * TOK)

    def key_slot(slot):
        return key_t.at[:, 0:HEAD_DIM, columns(slot)]

    def value_slot(slot):
        return value_t.at[:, 0:HEAD_DIM, columns(slot)]

    load_feature = fetch(feature, raw.at[h, 0:TOK], 0)
    load_prev = fetch(prev_feature, prev_in, 1)
    load_keys = fetch(prev_keys, key_slot(0), 2)
    load_values = fetch(prev_values, value_slot(0), 3)
    load_conv = fetch(conv_weight, conv_w, 4)
    load_q = fetch(w_query, qkv_w.at[0], 5)
    load_k = fetch(w_key, qkv_w.at[1], 6)
    load_v = fetch(w_value, qkv_w.at[2], 7)
    load_o = fetch(w_out, out_w, 8)

    barrier = pltpu.get_barrier_semaphore()
    peers = [dev_chip, dev_far, dev_diag, dev_up, dev_down]
    peers += key_peers + query_peers + rim_peers
    for peer in peers:
        pl.semaphore_signal(barrier, inc=1, device_id=peer, device_id_type=MESH)

    load_prev.wait()
    stale = prev_in[...].astype(F32)
    sums_own[0] = jnp.zeros((8, WIDTH), F32)
    sums_own[0, 0:1] = jnp.sum(stale, axis=0, keepdims=True)
    sums_own[0, 1:2] = jnp.sum(stale * stale, axis=0, keepdims=True)
    key_t[:, HEAD_DIM : 2 * HEAD_DIM, :] = jnp.zeros((HEADS_DEV, HEAD_DIM, 9 * TOK), BF16)
    query_heads[...] = jnp.zeros(query_heads.shape, BF16)
    value_t[:, HEAD_DIM : 2 * HEAD_DIM, :] = jnp.ones((HEADS_DEV, HEAD_DIM, 9 * TOK), BF16)
    load_o.wait()
    for i in range(4):
        out_w_send[i] = out_w[:, i * WIDTH : (i + 1) * WIDTH].T
    out_w_rows[h] = out_w_send[h]
    load_feature.wait()
    load_keys.wait()
    load_values.wait()

    row_group = (lax.broadcasted_iota(jnp.int32, (WIDTH, WIDTH), 0) * 1639) >> 16
    col_group = (lax.broadcasted_iota(jnp.int32, (WIDTH, WIDTH), 1) * 1639) >> 16
    same_group = jnp.where(row_group == col_group, 1.0, 0.0).astype(F32)
    groups[...] = same_group
    pl.semaphore_wait(barrier, len(peers))

    def relay_start(up, down, relay_up, relay_down, sem):
        push(up, relay_up, sem, dev_up)
        push(down, relay_down, sem + 1, dev_down)

    def relay_on(relay_up, relay_down, far_up, far_down, sem):
        arrived(relay_up, sem, dev_down)
        push(relay_up, far_up, sem + 2, dev_up)
        arrived(relay_down, sem + 1, dev_up)
        push(relay_down, far_down, sem + 3, dev_down)

    def relay_end(up, down, whole, sem):
        arrived(up, sem + 2, dev_down)
        arrived(down, sem + 3, dev_up)
        push(whole, whole, sem + 5, dev_chip)

    half = TOK // 2

    for i, peer in enumerate(key_peers):
        push(sums_own.at[0], sums_key.at[i], SEM_STATS_KEY + i, peer)

    relay_start(
        raw.at[h, 0:half],
        raw.at[h, half:TOK],
        relay_feature.at[0],
        relay_feature.at[1],
        SEM_FEATURE,
    )
    push(raw.at[h, 0:TOK], raw.at[h, 0:TOK], SEM_FEATURE + 4, dev_chip)
    above, below = slice(TOK, TOK + COLS), slice(TOK + COLS, TOK + 2 * COLS)
    for i in range(2):
        push(prev_in.at[TOK - COLS : TOK], raw.at[h, above], SEM_ROWS + i, rim_peers[i])
        push(prev_in.at[0:COLS], raw.at[h, below], SEM_ROWS + 2 + i, rim_peers[2 + i])

    total = sums_own[0]
    for i, peer in enumerate(key_peers):
        arrived(sums_key.at[i], SEM_STATS_KEY + i, peer)
        total = total + sums_key[i]
    sums_own[1] = total
    for i, peer in enumerate(query_peers):
        push(sums_own.at[1], sums_query.at[i], SEM_STATS_QUERY + i, peer)

    for i, peer in enumerate(query_peers):
        arrived(sums_query.at[i], SEM_STATS_QUERY + i, peer)
        total = total + sums_query[i]
    sums_head[h] = total
    head_peers = ((dev_chip, h_chip), (dev_far, h_far), (dev_diag, h_diag))
    for i, (peer, other) in enumerate(head_peers):
        push(sums_head.at[h], sums_head.at[h], SEM_STATS_HEAD + i, peer)

    def push_key(src, slot, device):
        push(src, key_slot(slot), SEM_KEY + slot, device)

    def push_value(src, slot, device):
        push(src, value_slot(slot), SEM_VALUE + slot, device)

    for slot, peer in ((3, dev_xf), (2, dev_y1), (1, dev_y3)):
        push_key(key_slot(0), slot, peer)
        push_value(value_slot(0), slot, peer)

    relay_on(
        relay_feature.at[0],
        relay_feature.at[1],
        raw.at[h_down, 0:half],
        raw.at[h_up, half:TOK],
        SEM_FEATURE,
    )
    for i, other in enumerate((h, h_far)):
        arrived(raw.at[other, above], SEM_ROWS + i, rim_peers[2 + i])
        arrived(raw.at[other, below], SEM_ROWS + 2 + i, rim_peers[i])
        rims = raw.at[other, TOK : TOK + 2 * COLS]
        push(rims, rims, SEM_RIMS + i, dev_chip)

    for i, (peer, other) in enumerate(head_peers):
        arrived(sums_head.at[other], SEM_STATS_HEAD + i, peer)
    group_sums = (
        jnp.dot(
            sums_head[...].reshape(32, WIDTH),
            groups[...],
            precision=lax.Precision.HIGHEST,
            preferred_element_type=F32,
        )
        * (1.0 / COUNT)
    )

    for i in range(4):
        centre = group_sums[8 * i : 8 * i + 1]
        square = group_sums[8 * i + 1 : 8 * i + 2]
        rstd = 0.5 * lax.rsqrt(square - centre * centre + 1e-05)
        slopes[i, 0:1] = rstd
        slopes[i, 1:2] = -centre * rstd

    def rims_of(other):
        return raw.at[other, TOK : TOK + 2 * COLS]

    arrived(rims_of(h_chip), SEM_RIMS, dev_chip)
    arrived(raw.at[h_chip, 0:TOK], SEM_FEATURE + 4, dev_chip)

    def activate(chip, place, src, dst, rows, inside):
        for c in range(2):
            i = chip * 2 + c
            v = raw[i, pl.ds(src, rows)].astype(F32) * slopes[i, 0:1] + slopes[i, 1:2]
            v = v + v * jnp.tanh(v)
            if inside is not None:
                v = jnp.where(inside, v, 0.0)
            act[place, pl.ds(dst, rows), c * WIDTH : (c + 1) * WIDTH] = v.astype(BF16)

    def activate_chip(chip, place):
        def body(t, carry):
            first = pl.multiple_of(t * 48, 48)
            activate(chip, place, first, pl.multiple_of(first + COLS, 48), 48, None)
            return carry

        lax.fori_loop(0, 8, body, 0)
        activate(chip, place, TOK, 0, COLS, p > 0)
        activate(chip, place, TOK + COLS, TOK + COLS, COLS, p < N_PATCH - 1)

    def convolve(place, chip, first, count):
        channels = pl.ds(pl.multiple_of(chip * (C // 2), 128), C // 2)

        def body(dx, carry):
            total = None
            for dy in range(3):
                product = lax.dot_general(
                    act[place, first + dy * COLS : first + dy * COLS + count],
                    conv_w[dy * 3 + dx, :, channels],
                    NT,
                    preferred_element_type=F32,
                )
                total = product if total is None else total + product
            if place == 0:
                conv_part[dx, first : first + count] = total
            else:
                conv_part[dx, first : first + count] += total
            return carry

        lax.fori_loop(0, 3, body, 0)

    activate_chip(zh, 0)
    load_conv.wait()
    relay_end(raw.at[h_far, 0:half], raw.at[h_far, half:TOK], raw.at[h_far, 0:TOK], SEM_FEATURE)
    convolve(0, zh, 0, TOK)
    arrived(rims_of(h_diag), SEM_RIMS + 1, dev_chip)
    arrived(raw.at[h_diag, 0:TOK], SEM_FEATURE + 5, dev_chip)
    activate_chip(1 - zh, 1)

    def conv_half(part_of):
        first = part_of * half
        convolve(1, 1 - zh, first, half)

        def merge_body(t, carry):
            rows = pl.ds(pl.multiple_of(t * COLS, COLS), COLS)
            col = lax.broadcasted_iota(jnp.int32, (COLS, WIDTH), 0)
            left = jnp.where(col == 0, 0.0, pltpu.roll(conv_part[0, rows], 1, axis=0))
            right = jnp.where(
                col == COLS - 1, 0.0, pltpu.roll(conv_part[2, rows], COLS - 1, axis=0)
            )
            result = raw[h, rows].astype(F32) + (conv_part[1, rows] + left + right)
            res_out[rows] = result
            tokens[h, rows] = result.astype(BF16)
            return carry

        lax.fori_loop(2 * part_of, 2 * part_of + 2, merge_body, 0)
        middle, last = first + COLS, first + half
        sem = SEM_TOKENS + 6 * part_of
        relay_start(
            tokens.at[h, first:middle],
            tokens.at[h, middle:last],
            relay_tokens.at[0, part_of],
            relay_tokens.at[1, part_of],
            sem,
        )
        push(tokens.at[h, first:last], tokens.at[h, first:last], sem + 4, dev_chip)

    def tokens_on(part_of):
        first, middle = part_of * half, part_of * half + COLS
        relay_on(
            relay_tokens.at[0, part_of],
            relay_tokens.at[1, part_of],
            tokens.at[h_down, first:middle],
            tokens.at[h_up, middle : first + half],
            SEM_TOKENS + 6 * part_of,
        )

    def tokens_end(part_of):
        first, middle, last = part_of * half, part_of * half + COLS, part_of * half + half
        relay_end(
            tokens.at[h_far, first:middle],
            tokens.at[h_far, middle:last],
            tokens.at[h_far, first:last],
            SEM_TOKENS + 6 * part_of,
        )

    def tokens_come(part_of):
        rows, sem = slice(part_of * half, part_of * half + half), SEM_TOKENS + 6 * part_of
        arrived(tokens.at[h_chip, rows], sem + 4, dev_chip)
        arrived(tokens.at[h_diag, rows], sem + 5, dev_chip)

    conv_half(0)
    arrived(key_slot(2), SEM_KEY + 2, dev_y3)
    push_key(key_slot(2), 4, dev_y1)
    arrived(value_slot(1), SEM_VALUE + 1, dev_y1)
    push_value(value_slot(1), 4, dev_y3)
    conv_half(1)
    store_resnet = fetch(res_out, resnet_ref, 9)
    tokens_on(0)
    arrived(key_slot(3), SEM_KEY + 3, dev_xf)
    push_key(key_slot(3), 6, dev_y1)
    push_key(key_slot(3), 5, dev_y3)
    arrived(value_slot(3), SEM_VALUE + 3, dev_xf)
    push_value(value_slot(3), 6, dev_y1)
    push_value(value_slot(3), 5, dev_y3)
    tokens_on(1)
    tokens_end(0)
    tokens_end(1)
    tokens_come(0)
    tokens_come(1)

    def norm_body(t, carry):
        rows = pl.ds(pl.multiple_of(t * COLS, COLS), COLS)
        parts = [tokens[i, rows].astype(F32) for i in range(4)]
        mean = sum(jnp.sum(v, axis=1, keepdims=True) for v in parts) * (1.0 / C)
        square = sum(jnp.sum(v * v, axis=1, keepdims=True) for v in parts) * (1.0 / C)
        rstd = lax.rsqrt(square - mean * mean + 1e-05)
        for i in range(4):
            normed[rows, i * WIDTH : (i + 1) * WIDTH] = ((parts[i] - mean) * rstd).astype(BF16)
        return carry

    lax.fori_loop(0, 4, norm_body, 0)

    def split_heads(slot):
        for i in range(HEADS_DEV):
            query_heads[slot, i, :, 0:HEAD_DIM] = queries[slot, i].T

    def project_tokens(i):
        result = lax.dot_general(qkv_w[i], normed[...], NT, preferred_element_type=F32)
        return result.astype(BF16).reshape(HEADS_DEV, HEAD_DIM, TOK)

    load_q.wait()
    queries[0] = project_tokens(0)
    for i, peer in enumerate(query_peers[:2]):
        push(queries.at[0], queries.at[i + 1], SEM_QUERY + i, peer)
    load_k.wait()
    key_t[:, 0:HEAD_DIM, 0:TOK] = project_tokens(1)
    load_v.wait()
    value_t[:, 0:HEAD_DIM, 0:TOK] = project_tokens(2)
    split_heads(0)

    lane = lax.broadcasted_iota(jnp.int32, (128, 128), 1)

    def score_rows(slot, first, i, t):
        rows = slice(t * 128, (t + 1) * 128)
        result = jnp.dot(
            query_heads[slot, i, rows],
            key_t[i, :, first : first + CHUNK],
            preferred_element_type=F32,
        )
        scores[t] = result
        tops[t] = functools.reduce(
            jnp.maximum, [result[:, 128 * k : 128 * (k + 1)] for k in range(CHUNK // 128)]
        )

    def weigh_rows(slot, first, i, t):
        rows = slice(t * 128, (t + 1) * 128)
        top = jnp.max(tops[t], axis=1, keepdims=True) * SCORE_SCALE
        weights = jnp.exp2(scores[t] * SCORE_SCALE - top).astype(BF16)
        summed = lax.dot_general(
            weights, value_t[i, :, first : first + CHUNK], NT, preferred_element_type=F32
        )
        turned = jnp.where(lane == 65, top, summed).T
        if first != SECOND:
            part[slot, i, :, rows] = turned[0:72]
            return
        before = part[slot, i, :, rows]
        level = jnp.maximum(before[65:66], turned[65:66])
        both = before[0:65] * jnp.exp2(before[65:66] - level) + turned[0:65] * jnp.exp2(
            turned[65:66] - level
        )
        result = both[0:64] / both[64:65]
        lse = level + jnp.log2(both[64:65])
        if slot == 0:
            part[0, i, 0:64, rows] = result
        else:
            partial_out[slot - 1, i, :, rows] = result.astype(BF16)
        level_out[slot, i, :, rows] = jnp.broadcast_to(lse, (8, 128))

    def partial_copies(slot, i):
        n = (slot - 1) * HEADS_DEV + i
        return (
            copy(
                partial_out.at[slot - 1, i],
                partial_in.at[slot - 1, i],
                SEM_PARTIAL + n,
                SEM_PARTIAL + n,
                query_peers[slot - 1],
            ),
            copy(
                level_out.at[slot, i],
                level_in.at[slot - 1, i],
                SEM_LEVEL + n,
                SEM_LEVEL + n,
                query_peers[slot - 1],
            ),
        )

    def send_partial(slot, first, i):
        if slot > 0 and first == SECOND:
            for c in partial_copies(slot, i):
                c.start()

    steps = [(0, FIRST_OWN)]
    steps += [(slot, FIRST_OTHER) for slot in (1, 2, 3)]
    steps += [(slot, SECOND) for slot in (3, 2, 1, 0)]

    def attend(step):
        slot, first = steps[step]

        def body(i, carry):
            score_rows(slot, first, i, 1)
            weigh_rows(slot, first, i, 0)
            score_rows(slot, first, i, 2)
            weigh_rows(slot, first, i, 1)
            score_rows(slot, first, i + 1, 0)
            weigh_rows(slot, first, i, 2)
            send_partial(slot, first, i)
            return carry

        lax.fori_loop(0, HEADS_DEV - 1, body, 0)

    def attend_head(slot, first, i, following):
        def body(unused, carry):
            score_rows(slot, first, i, 1)
            weigh_rows(slot, first, i, 0)
            score_rows(slot, first, i, 2)
            weigh_rows(slot, first, i, 1)
            if following is not None:
                score_rows(*following, 0)
            weigh_rows(slot, first, i, 2)
            send_partial(slot, first, i)
            return carry

        lax.fori_loop(0, 1, body, 0)

    def attend_last(step):
        attend_head(*steps[step], HEADS_DEV - 1, (*steps[step + 1], 0))

    def combine(i):
        for r in range(3):
            for c in partial_copies(r + 1, i):
                c.wait_recv()
        levels = [level_out[0, i, 0:1]] + [level_in[r, i, 0:1] for r in range(3)]
        top = functools.reduce(jnp.maximum, levels)
        shares = [jnp.exp2(level - top) for level in levels]
        whole = 1.0 / sum(shares)
        result = part[0, i, 0:64] * (shares[0] * whole)
        for r in range(3):
            result = result + partial_in[r, i].astype(F32) * (shares[r + 1] * whole)
        heads[h, i] = result.astype(BF16)
        push(heads.at[h, i], relay_heads.at[i], SEM_HEADS + i, dev_down if i % 2 else dev_up)
        push(heads.at[h, i], heads.at[h, i], SEM_HEADS + 10 + i, dev_chip)

    def heads_on(i):
        source, target = (dev_up, dev_down) if i % 2 else (dev_down, dev_up)
        arrived(relay_heads.at[i], SEM_HEADS + i, source)
        far = heads.at[h_up if i % 2 else h_down, i]
        push(relay_heads.at[i], far, SEM_HEADS + 5 + i, target)

    def heads_end(i):
        far = heads.at[h_far, i]
        arrived(far, SEM_HEADS + 5 + i, dev_up if i % 2 else dev_down)
        push(far, far, SEM_HEADS + 15 + i, dev_chip)

    arrived(key_slot(1), SEM_KEY + 1, dev_y1)
    arrived(value_slot(2), SEM_VALUE + 2, dev_y3)
    score_rows(0, FIRST_OWN, 0, 0)
    attend(0)
    arrived(key_slot(6), SEM_KEY + 6, dev_y3)
    push_key(key_slot(6), 7, dev_y1)
    arrived(value_slot(5), SEM_VALUE + 5, dev_y1)
    push_value(value_slot(5), 7, dev_y3)
    push(queries.at[0], queries.at[3], SEM_QUERY + 2, query_peers[2])

    for step in range(1, 4):
        arrived(queries.at[step], SEM_QUERY + step - 1, query_peers[step - 1])
        split_heads(step)
        attend_last(step - 1)
        attend(step)
        if step == 2:
            for i, (peer, other) in enumerate(head_peers):
                push(out_w_send.at[other], out_w_rows.at[h], SEM_W_OUT + i, peer)

    arrived(key_slot(5), SEM_KEY + 5, dev_y1)
    arrived(value_slot(6), SEM_VALUE + 6, dev_y3)
    arrived(key_slot(4), SEM_KEY + 4, dev_y3)
    arrived(value_slot(4), SEM_VALUE + 4, dev_y1)
    arrived(key_slot(7), SEM_KEY + 7, dev_y3)
    arrived(value_slot(7), SEM_VALUE + 7, dev_y1)

    for step in range(4, 7):
        attend_last(step - 1)
        attend(step)
    attend_last(6)
    for i in range(HEADS_DEV):
        attend_head(0, SECOND, i, (0, SECOND, i + 1) if i + 1 < HEADS_DEV else None)
        combine(i)
        if i > 0:
            heads_on(i - 1)
        if i > 1:
            heads_end(i - 2)
    heads_on(HEADS_DEV - 1)
    heads_end(HEADS_DEV - 2)

    for i, (peer, other) in enumerate(head_peers):
        arrived(out_w_rows.at[other], SEM_W_OUT + i, peer)

    def project(i):
        return jnp.dot(
            out_w_rows[i], heads[i].reshape(WIDTH, TOK), preferred_element_type=F32
        )

    attended[...] = project(h)
    for i in range(HEADS_DEV):
        arrived(heads.at[h_chip, i], SEM_HEADS + 10 + i, dev_chip)
    attended[...] += project(h_chip)
    heads_end(HEADS_DEV - 1)
    attended[...] += project(h_far)
    for i in range(HEADS_DEV):
        arrived(heads.at[h_diag, i], SEM_HEADS + 15 + i, dev_chip)
    attended[...] += project(h_diag)
    store_attended = fetch(attended, attended_ref, 10)

    for c in started:
        c.wait_send()
    for slot in range(1, 4):
        for i in range(HEADS_DEV):
            for c in partial_copies(slot, i):
                c.wait_send()
    store_resnet.wait()
    store_attended.wait()


def on_device(
    feature, prev_feature, conv_weight, w_query, w_key, w_value, w_out, prev_keys, prev_values
):
    any_spec = pl.BlockSpec(memory_space=pl.ANY)
    vmem = pltpu.VMEM
    scratch = [
        vmem((4, TOK + 2 * COLS, WIDTH), BF16),
        vmem((TOK, WIDTH), BF16),
        vmem((2, 8, WIDTH), F32),
        vmem((7, 8, WIDTH), F32),
        vmem((3, 8, WIDTH), F32),
        vmem((4, 8, WIDTH), F32),
        vmem((WIDTH, WIDTH), F32),
        vmem((4, 8, WIDTH), F32),
        vmem((2, TOK + 2 * COLS, C // 2), BF16),
        vmem((9, WIDTH, C), BF16),
        vmem((3, WIDTH, C), BF16),
        vmem((3, TOK, WIDTH), F32),
        vmem((TOK, WIDTH), F32),
        vmem((4, TOK, WIDTH), BF16),
        vmem((TOK, C), BF16),
        vmem((4, HEADS_DEV, HEAD_DIM, TOK), BF16),
        vmem((4, HEADS_DEV, TOK, 2 * HEAD_DIM), BF16),
        vmem((HEADS_DEV, 2 * HEAD_DIM, 9 * TOK), BF16),
        vmem((HEADS_DEV, 2 * HEAD_DIM, 9 * TOK), BF16),
        vmem((3, 128, CHUNK), F32),
        vmem((3, 128, 128), F32),
        vmem((4, HEADS_DEV, 72, TOK), F32),
        vmem((3, HEADS_DEV, HEAD_DIM, TOK), BF16),
        vmem((3, HEADS_DEV, HEAD_DIM, TOK), BF16),
        vmem((4, HEADS_DEV, 8, TOK), F32),
        vmem((3, HEADS_DEV, 8, TOK), F32),
        vmem((2, TOK // 2, WIDTH), BF16),
        vmem((2, 2, COLS, WIDTH), BF16),
        vmem((HEADS_DEV, HEAD_DIM, TOK), BF16),
        vmem((4, HEADS_DEV, HEAD_DIM, TOK), BF16),
        vmem((WIDTH, C), BF16),
        vmem((4, WIDTH, WIDTH), BF16),
        vmem((4, WIDTH, WIDTH), BF16),
        vmem((WIDTH, TOK), F32),
        pltpu.SemaphoreType.DMA((SEMS,)),
        pltpu.SemaphoreType.DMA((SEMS,)),
        pltpu.SemaphoreType.DMA((11,)),
    ]
    resnet_out, attended = pl.pallas_call(
        kernel,
        out_shape=(
            jax.ShapeDtypeStruct((TOK, WIDTH), F32),
            jax.ShapeDtypeStruct((WIDTH, TOK), F32),
        ),
        in_specs=[any_spec] * 9,
        out_specs=(any_spec, any_spec),
        scratch_shapes=scratch,
        compiler_params=pltpu.CompilerParams(
            collective_id=0, has_side_effects=True, vmem_limit_bytes=60 * 2**20
        ),
    )(
        feature.reshape(TOK, WIDTH),
        prev_feature.reshape(TOK, WIDTH),
        conv_weight.reshape(9, C, WIDTH).transpose(0, 2, 1),
        w_query.T,
        w_key.T,
        w_value.T,
        w_out,
        prev_keys.T.reshape(HEADS_DEV, HEAD_DIM, TOK),
        prev_values.T.reshape(HEADS_DEV, HEAD_DIM, TOK),
    )
    return (resnet_out.reshape(feature.shape), attended.T)


def solution(mesh):
    placed = (
        P("patch", None, "head"),
        P("patch", None, "head"),
        P(None, None, None, "head"),
        P(None, "head"),
        P(None, "head"),
        P(None, "head"),
        P("head", None),
        P("patch", "head"),
        P("patch", "head"),
    )
    return jax.shard_map(
        on_device,
        mesh=mesh,
        in_specs=placed,
        out_specs=(P("patch", None, "head"), P("patch", "head")),
        check_vma=False,
    )
```

```python
import functools

import jax
import jax.numpy as jnp
from jax import lax
from jax.experimental import pallas as pl
from jax.experimental.pallas import tpu as pltpu
from jax.sharding import PartitionSpec as P

C = 1280
GROUPS = 32
HEAD_DIM = 64
TOK = 384
COLS = 96
WIDTH = 320
HEADS_DEV = 5
CHUNK = 4 * TOK
FIRST_OWN = 0
FIRST_OTHER = TOK
SECOND = 5 * TOK
PLACE = {0: 4, 1: 1, 2: 2, 3: 3, 4: 5, 5: 6, 6: 7, 7: 8}
NT = (((1,), (1,)), ((), ()))
N_PATCH = 32
COUNT = 128 * 96 * (C // GROUPS)
SCORE_SCALE = 1.4426950408889634 / HEAD_DIM**0.5
BF16 = jnp.bfloat16
F32 = jnp.float32
MESH = pl.DeviceIdType.MESH

SEM_FEATURE = 0
SEM_ROWS = 6
SEM_RIMS = 10
SEM_TOKENS = 12
SEM_W_OUT = 24
SEM_STATS_HEAD = 27
SEM_STATS_KEY = 30
SEM_STATS_QUERY = 37
SEM_QUERY = 40
SEM_KEY = 43
SEM_VALUE = 51
SEM_PARTIAL = 59
SEM_HEADS = 65
SEMS = 77


def kernel(
    feature,
    prev_feature,
    conv_weight,
    w_query,
    w_key,
    w_value,
    w_out,
    prev_keys,
    prev_values,
    resnet_ref,
    attended_ref,
    raw,
    prev_in,
    sums_own,
    sums_key,
    sums_query,
    sums_head,
    groups,
    slopes,
    act,
    conv_w,
    qkv_w,
    conv_part,
    res_out,
    tokens,
    normed,
    queries,
    query_heads,
    key_t,
    value_t,
    scores,
    tops,
    part,
    partial_out,
    partial_in,
    relay_feature,
    relay_tokens,
    relay_heads,
    heads,
    out_w,
    out_w_send,
    out_w_rows,
    attended,
    send,
    recv,
    local,
):
    p = lax.axis_index("patch")
    h = lax.axis_index("head")
    x, y, zl = p // 8, (p // 2) % 4, p % 2

    def at(xx, yy, zz):
        return xx * 8 + yy * 2 + zz

    xn = x + 1 - 2 * (x % 2)
    xf = (x + 2) % 4
    y1, y2, y3 = (y + 1) % 4, (y + 2) % 4, (y + 3) % 4
    zh, core = h // 2, h % 2
    h_chip = zh * 2 + 1 - core
    h_far = (1 - zh) * 2 + core
    h_diag = (1 - zh) * 2 + 1 - core
    h_up = ((zh + zl) % 2) * 2 + core
    h_down = ((zh + 1 - zl) % 2) * 2 + core

    dev_chip, dev_far, dev_diag = (p, h_chip), (p, h_far), (p, h_diag)
    dev_up, dev_down = (at(x, y, 1 - zl), h_up), (at(x, y, 1 - zl), h_down)
    key_peers = [
        (at(x, y1, zl), h),
        (at(x, y3, zl), h),
        (at(x, y2, zl), h),
        (at(xf, y, zl), h),
        (at(xf, y1, zl), h),
        (at(xf, y3, zl), h),
        (at(xf, y2, zl), h),
    ]
    dev_y1, dev_y3, dev_y2, dev_xf = key_peers[:4]
    query_peers = [(at(x, y, 1 - zl), h), (at(xn, y, zl), h), (at(xn, y, 1 - zl), h)]
    p_next, p_prev = (p + 1) % N_PATCH, (p + N_PATCH - 1) % N_PATCH
    rim_peers = [(p_next, h), (p_next, h_far), (p_prev, h), (p_prev, h_far)]

    started = []

    def copy(src, dst, sem_send, sem_recv, device):
        return pltpu.make_async_remote_copy(
            src_ref=src,
            dst_ref=dst,
            send_sem=send.at[sem_send],
            recv_sem=recv.at[sem_recv],
            device_id=device,
            device_id_type=MESH,
        )

    def push(src, dst, sem, device, sem_send=None):
        c = copy(src, dst, sem if sem_send is None else sem_send, sem, device)
        c.start()
        started.append(c)

    def arrived(dst, sem, device):
        copy(dst, dst, sem, sem, device).wait_recv()

    def fetch(src, dst, sem):
        c = pltpu.make_async_copy(src, dst, local.at[sem])
        c.start()
        return c

    def columns(slot):
        return slice(PLACE[slot] * TOK, (PLACE[slot] + 1) * TOK)

    def key_slot(slot):
        return key_t.at[:, 0:HEAD_DIM, columns(slot)]

    def value_slot(slot):
        return value_t.at[:, 0:HEAD_DIM, columns(slot)]

    load_feature = fetch(feature, raw.at[h, 0:TOK], 0)
    load_prev = fetch(prev_feature, prev_in, 1)
    load_keys = fetch(prev_keys, key_slot(0), 2)
    load_values = fetch(prev_values, value_slot(0), 3)
    load_conv = fetch(conv_weight, conv_w, 4)
    load_q = fetch(w_query, qkv_w.at[0], 5)
    load_k = fetch(w_key, qkv_w.at[1], 6)
    load_v = fetch(w_value, qkv_w.at[2], 7)
    load_o = fetch(w_out, out_w, 8)

    barrier = pltpu.get_barrier_semaphore()
    peers = [dev_chip, dev_far, dev_diag, dev_up, dev_down]
    peers += key_peers + query_peers + rim_peers
    for peer in peers:
        pl.semaphore_signal(barrier, inc=1, device_id=peer, device_id_type=MESH)

    load_prev.wait()
    stale = prev_in[...].astype(F32)
    sums_own[0] = jnp.zeros((8, WIDTH), F32)
    sums_own[0, 0:1] = jnp.sum(stale, axis=0, keepdims=True)
    sums_own[0, 1:2] = jnp.sum(stale * stale, axis=0, keepdims=True)
    value_t[:, HEAD_DIM : 2 * HEAD_DIM, :] = jnp.ones((HEADS_DEV, HEAD_DIM, 9 * TOK), BF16)
    load_o.wait()
    for i in range(4):
        out_w_send[i] = out_w[:, i * WIDTH : (i + 1) * WIDTH].T
    out_w_rows[h] = out_w_send[h]
    load_feature.wait()
    load_keys.wait()
    load_values.wait()

    def repeat_keys(cols):
        key_t[:, HEAD_DIM : 2 * HEAD_DIM, cols] = key_t[:, 0:HEAD_DIM, cols]

    repeat_keys(columns(0))

    row_group = (lax.broadcasted_iota(jnp.int32, (WIDTH, WIDTH), 0) * 1639) >> 16
    col_group = (lax.broadcasted_iota(jnp.int32, (WIDTH, WIDTH), 1) * 1639) >> 16
    same_group = jnp.where(row_group == col_group, 1.0, 0.0).astype(F32)
    groups[...] = same_group
    pl.semaphore_wait(barrier, len(peers))

    def relay_start(up, down, relay_up, relay_down, sem):
        push(up, relay_up, sem, dev_up)
        push(down, relay_down, sem + 1, dev_down)

    def relay_on(relay_up, relay_down, far_up, far_down, sem):
        arrived(relay_up, sem, dev_down)
        push(relay_up, far_up, sem + 2, dev_up)
        arrived(relay_down, sem + 1, dev_up)
        push(relay_down, far_down, sem + 3, dev_down)

    def relay_end(up, down, whole, sem):
        arrived(up, sem + 2, dev_down)
        arrived(down, sem + 3, dev_up)
        push(whole, whole, sem + 5, dev_chip)

    half = TOK // 2

    for i, peer in enumerate(key_peers):
        push(sums_own.at[0], sums_key.at[i], SEM_STATS_KEY + i, peer)

    relay_start(
        raw.at[h, 0:half],
        raw.at[h, half:TOK],
        relay_feature.at[0],
        relay_feature.at[1],
        SEM_FEATURE,
    )
    push(raw.at[h, 0:TOK], raw.at[h, 0:TOK], SEM_FEATURE + 4, dev_chip)
    above, below = slice(TOK, TOK + COLS), slice(TOK + COLS, TOK + 2 * COLS)
    for i in range(2):
        push(prev_in.at[TOK - COLS : TOK], raw.at[h, above], SEM_ROWS + i, rim_peers[i])
        push(prev_in.at[0:COLS], raw.at[h, below], SEM_ROWS + 2 + i, rim_peers[2 + i])

    total = sums_own[0]
    for i, peer in enumerate(key_peers):
        arrived(sums_key.at[i], SEM_STATS_KEY + i, peer)
        total = total + sums_key[i]
    sums_own[1] = total
    for i, peer in enumerate(query_peers):
        push(sums_own.at[1], sums_query.at[i], SEM_STATS_QUERY + i, peer)

    for i, peer in enumerate(query_peers):
        arrived(sums_query.at[i], SEM_STATS_QUERY + i, peer)
        total = total + sums_query[i]
    sums_head[h] = total
    head_peers = ((dev_chip, h_chip), (dev_far, h_far), (dev_diag, h_diag))
    for i, (peer, other) in enumerate(head_peers):
        push(sums_head.at[h], sums_head.at[h], SEM_STATS_HEAD + i, peer)

    def push_key(src, slot, device):
        push(src, key_slot(slot), SEM_KEY + slot, device)

    def push_value(src, slot, device):
        push(src, value_slot(slot), SEM_VALUE + slot, device)

    for slot, peer in ((3, dev_xf), (2, dev_y1), (1, dev_y3)):
        push_key(key_slot(0), slot, peer)
        push_value(value_slot(0), slot, peer)

    relay_on(
        relay_feature.at[0],
        relay_feature.at[1],
        raw.at[h_down, 0:half],
        raw.at[h_up, half:TOK],
        SEM_FEATURE,
    )
    for i, other in enumerate((h, h_far)):
        arrived(raw.at[other, above], SEM_ROWS + i, rim_peers[2 + i])
        arrived(raw.at[other, below], SEM_ROWS + 2 + i, rim_peers[i])
        rims = raw.at[other, TOK : TOK + 2 * COLS]
        push(rims, rims, SEM_RIMS + i, dev_chip)

    for i, (peer, other) in enumerate(head_peers):
        arrived(sums_head.at[other], SEM_STATS_HEAD + i, peer)
    group_sums = (
        jnp.dot(
            sums_head[...].reshape(32, WIDTH),
            groups[...],
            precision=lax.Precision.HIGHEST,
            preferred_element_type=F32,
        )
        * (1.0 / COUNT)
    )

    for i in range(4):
        centre = group_sums[8 * i : 8 * i + 1]
        square = group_sums[8 * i + 1 : 8 * i + 2]
        rstd = 0.5 * lax.rsqrt(square - centre * centre + 1e-05)
        slopes[i, 0:1] = rstd
        slopes[i, 1:2] = -centre * rstd

    def rims_of(other):
        return raw.at[other, TOK : TOK + 2 * COLS]

    arrived(rims_of(h_chip), SEM_RIMS, dev_chip)
    arrived(raw.at[h_chip, 0:TOK], SEM_FEATURE + 4, dev_chip)

    def activate(chip, place, src, dst, rows, inside):
        for c in range(2):
            i = chip * 2 + c
            v = raw[i, pl.ds(src, rows)].astype(F32) * slopes[i, 0:1] + slopes[i, 1:2]
            v = v + v * jnp.tanh(v)
            if inside is not None:
                v = jnp.where(inside, v, 0.0)
            act[place, pl.ds(dst, rows), c * WIDTH : (c + 1) * WIDTH] = v.astype(BF16)

    def activate_chip(chip, place):
        def body(t, carry):
            first = pl.multiple_of(t * 48, 48)
            activate(chip, place, first, pl.multiple_of(first + COLS, 48), 48, None)
            return carry

        lax.fori_loop(0, 8, body, 0)
        activate(chip, place, TOK, 0, COLS, p > 0)
        activate(chip, place, TOK + COLS, TOK + COLS, COLS, p < N_PATCH - 1)

    def convolve(place, chip, first, count):
        channels = pl.ds(pl.multiple_of(chip * (C // 2), 128), C // 2)

        def body(dx, carry):
            total = None
            for dy in range(3):
                product = lax.dot_general(
                    act[place, first + dy * COLS : first + dy * COLS + count],
                    conv_w[dy * 3 + dx, :, channels],
                    NT,
                    preferred_element_type=F32,
                )
                total = product if total is None else total + product
            if place == 0:
                conv_part[dx, first : first + count] = total
            else:
                conv_part[dx, first : first + count] += total
            return carry

        lax.fori_loop(0, 3, body, 0)

    activate_chip(zh, 0)
    load_conv.wait()
    relay_end(raw.at[h_far, 0:half], raw.at[h_far, half:TOK], raw.at[h_far, 0:TOK], SEM_FEATURE)
    convolve(0, zh, 0, TOK)
    arrived(rims_of(h_diag), SEM_RIMS + 1, dev_chip)
    arrived(raw.at[h_diag, 0:TOK], SEM_FEATURE + 5, dev_chip)
    activate_chip(1 - zh, 1)

    def conv_half(part_of):
        first = part_of * half
        convolve(1, 1 - zh, first, half)

        def merge_body(t, carry):
            rows = pl.ds(pl.multiple_of(t * COLS, COLS), COLS)
            col = lax.broadcasted_iota(jnp.int32, (COLS, WIDTH), 0)
            left = jnp.where(col == 0, 0.0, pltpu.roll(conv_part[0, rows], 1, axis=0))
            right = jnp.where(
                col == COLS - 1, 0.0, pltpu.roll(conv_part[2, rows], COLS - 1, axis=0)
            )
            result = raw[h, rows].astype(F32) + (conv_part[1, rows] + left + right)
            res_out[rows] = result
            tokens[h, rows] = result.astype(BF16)
            return carry

        lax.fori_loop(2 * part_of, 2 * part_of + 2, merge_body, 0)
        middle, last = first + COLS, first + half
        sem = SEM_TOKENS + 6 * part_of
        relay_start(
            tokens.at[h, first:middle],
            tokens.at[h, middle:last],
            relay_tokens.at[0, part_of],
            relay_tokens.at[1, part_of],
            sem,
        )
        push(tokens.at[h, first:last], tokens.at[h, first:last], sem + 4, dev_chip)

    def tokens_on(part_of):
        first, middle = part_of * half, part_of * half + COLS
        relay_on(
            relay_tokens.at[0, part_of],
            relay_tokens.at[1, part_of],
            tokens.at[h_down, first:middle],
            tokens.at[h_up, middle : first + half],
            SEM_TOKENS + 6 * part_of,
        )

    def tokens_end(part_of):
        first, middle, last = part_of * half, part_of * half + COLS, part_of * half + half
        relay_end(
            tokens.at[h_far, first:middle],
            tokens.at[h_far, middle:last],
            tokens.at[h_far, first:last],
            SEM_TOKENS + 6 * part_of,
        )

    def tokens_come(part_of):
        rows, sem = slice(part_of * half, part_of * half + half), SEM_TOKENS + 6 * part_of
        arrived(tokens.at[h_chip, rows], sem + 4, dev_chip)
        arrived(tokens.at[h_diag, rows], sem + 5, dev_chip)

    conv_half(0)
    arrived(key_slot(2), SEM_KEY + 2, dev_y3)
    push_key(key_slot(2), 4, dev_y1)
    arrived(value_slot(1), SEM_VALUE + 1, dev_y1)
    push_value(value_slot(1), 4, dev_y3)
    conv_half(1)
    store_resnet = fetch(res_out, resnet_ref, 9)
    tokens_on(0)
    arrived(key_slot(3), SEM_KEY + 3, dev_xf)
    push_key(key_slot(3), 6, dev_y1)
    push_key(key_slot(3), 5, dev_y3)
    arrived(value_slot(3), SEM_VALUE + 3, dev_xf)
    push_value(value_slot(3), 6, dev_y1)
    push_value(value_slot(3), 5, dev_y3)
    tokens_on(1)
    tokens_end(0)
    tokens_end(1)
    tokens_come(0)
    tokens_come(1)

    def norm_body(t, carry):
        rows = pl.ds(pl.multiple_of(t * COLS, COLS), COLS)
        parts = [tokens[i, rows].astype(F32) for i in range(4)]
        mean = sum(jnp.sum(v, axis=1, keepdims=True) for v in parts) * (1.0 / C)
        square = sum(jnp.sum(v * v, axis=1, keepdims=True) for v in parts) * (1.0 / C)
        rstd = lax.rsqrt(square - mean * mean + 1e-05)
        for i in range(4):
            normed[rows, i * WIDTH : (i + 1) * WIDTH] = ((parts[i] - mean) * rstd).astype(BF16)
        return carry

    lax.fori_loop(0, 4, norm_body, 0)

    def split_heads(slot):
        for i in range(HEADS_DEV):
            scaled = queries[slot, i].T.astype(F32) * SCORE_SCALE
            high = scaled.astype(BF16)
            low = (scaled - high.astype(F32)).astype(BF16)
            query_heads[slot, i, :, 0:HEAD_DIM] = high
            query_heads[slot, i, :, HEAD_DIM : 2 * HEAD_DIM] = low

    def project_tokens(i):
        result = lax.dot_general(qkv_w[i], normed[...], NT, preferred_element_type=F32)
        return result.astype(BF16).reshape(HEADS_DEV, HEAD_DIM, TOK)

    load_q.wait()
    queries[0] = project_tokens(0)
    for i, peer in enumerate(query_peers[:2]):
        push(queries.at[0], queries.at[i + 1], SEM_QUERY + i, peer)
    load_k.wait()
    key_t[:, 0:HEAD_DIM, 0:TOK] = project_tokens(1)
    repeat_keys(slice(0, TOK))
    load_v.wait()
    value_t[:, 0:HEAD_DIM, 0:TOK] = project_tokens(2)
    split_heads(0)

    lane = lax.broadcasted_iota(jnp.int32, (128, 128), 1)

    def score_rows(slot, first, i, t):
        rows = slice(t * 128, (t + 1) * 128)
        result = jnp.dot(
            query_heads[slot, i, rows],
            key_t[i, :, first : first + CHUNK],
            preferred_element_type=F32,
        )
        scores[t] = result
        tops[t] = functools.reduce(
            jnp.maximum, [result[:, 128 * k : 128 * (k + 1)] for k in range(CHUNK // 128)]
        )

    row_of = lax.broadcasted_iota(jnp.int32, (16, 128), 0)

    def weigh_rows(slot, first, i, t):
        rows = slice(t * 128, (t + 1) * 128)
        top = jnp.max(tops[t], axis=1, keepdims=True)
        weights = jnp.exp2(scores[t] - top).astype(BF16)
        summed = lax.dot_general(
            weights, value_t[i, :, first : first + CHUNK], NT, preferred_element_type=F32
        )
        turned = jnp.where(lane == 65, top, summed).T
        if first != SECOND:
            part[slot, i, :, rows] = turned[0:72]
            return
        before = part[slot, i, :, rows]
        level = jnp.maximum(before[65:66], turned[65:66])
        both = before[0:65] * jnp.exp2(before[65:66] - level) + turned[0:65] * jnp.exp2(
            turned[65:66] - level
        )
        if slot == 0:
            part[0, i, 0:64, rows] = both[0:64]
            part[0, i, 64:72, rows] = jnp.where(
                row_of[0:8] == 1, level, jnp.broadcast_to(both[64:65], (8, 128))
            )
            return
        lse = level + jnp.log2(both[64:65])
        high = lse.astype(BF16).astype(F32)
        middle = (lse - high).astype(BF16).astype(F32)
        pieces = jnp.where(row_of == 0, high, jnp.where(row_of == 1, middle, lse - high - middle))
        partial_out[slot - 1, i, 0:64, rows] = (both[0:64] / both[64:65]).astype(BF16)
        partial_out[slot - 1, i, 64:80, rows] = pieces.astype(BF16)

    steps = [(0, FIRST_OWN)]
    steps += [(slot, FIRST_OTHER) for slot in (1, 2, 3)]
    steps += [(slot, SECOND) for slot in (3, 2, 1, 0)]
    SPLITS = ((0, 3), (3, 5))

    def partial_copy(slot, part_of):
        n = (slot - 1) * 2 + part_of
        some = slice(*SPLITS[part_of])
        return copy(
            partial_out.at[slot - 1, some],
            partial_in.at[slot - 1, some],
            SEM_PARTIAL + n,
            SEM_PARTIAL + n,
            query_peers[slot - 1],
        )

    def attend(step, part_of):
        slot, first = steps[step]
        begin, end = SPLITS[part_of]

        def body(unused, carry):
            for i in range(begin, end):
                score_rows(slot, first, i, 1)
                weigh_rows(slot, first, i, 0)
                score_rows(slot, first, i, 2)
                weigh_rows(slot, first, i, 1)
                if i + 1 < HEADS_DEV:
                    score_rows(slot, first, i + 1, 0)
                elif step + 1 < len(steps):
                    score_rows(*steps[step + 1], 0, 0)
                weigh_rows(slot, first, i, 2)
            return carry

        lax.fori_loop(0, 1, body, 0)
        if slot > 0 and first == SECOND:
            partial_copy(slot, part_of).start()

    def combine(part_of):
        for r in range(3):
            partial_copy(r + 1, part_of).wait_recv()
        for i in range(*SPLITS[part_of]):
            last = part[0, i, 64:72]
            levels = [last[1:2]]
            for r in range(3):
                pieces = partial_in[r, i, 64:80].astype(F32)
                levels.append(pieces[0:1] + pieces[1:2] + pieces[2:3])
            top = functools.reduce(jnp.maximum, levels)
            shares = [jnp.exp2(level - top) for level in levels]
            whole = last[0:1] * shares[0]
            for share in shares[1:]:
                whole = whole + share
            whole = 1.0 / whole
            result = part[0, i, 0:64] * (shares[0] * whole)
            for r in range(3):
                result = result + partial_in[r, i, 0:64].astype(F32) * (shares[r + 1] * whole)
            heads[h, i] = result.astype(BF16)

    PIECES = ((slice(0, 3), True), (slice(3, 4), True), (slice(4, 5), False))

    def heads_start(n):
        some, upwards = PIECES[n]
        own = heads.at[h, some]
        push(own, relay_heads.at[some], SEM_HEADS + n, dev_up if upwards else dev_down)
        push(own, own, SEM_HEADS + 6 + n, dev_chip)

    def heads_on(n):
        some, upwards = PIECES[n]
        source, target = (dev_down, dev_up) if upwards else (dev_up, dev_down)
        arrived(relay_heads.at[some], SEM_HEADS + n, source)
        far = heads.at[h_down if upwards else h_up, some]
        push(relay_heads.at[some], far, SEM_HEADS + 3 + n, target)

    def heads_end(n):
        some, upwards = PIECES[n]
        far = heads.at[h_far, some]
        arrived(far, SEM_HEADS + 3 + n, dev_down if upwards else dev_up)
        push(far, far, SEM_HEADS + 9 + n, dev_chip)

    arrived(key_slot(1), SEM_KEY + 1, dev_y1)
    arrived(value_slot(2), SEM_VALUE + 2, dev_y3)
    for slot in range(1, 4):
        repeat_keys(columns(slot))
    score_rows(0, FIRST_OWN, 0, 0)
    attend(0, 0)
    arrived(key_slot(6), SEM_KEY + 6, dev_y3)
    push_key(key_slot(6), 7, dev_y1)
    arrived(value_slot(5), SEM_VALUE + 5, dev_y1)
    push_value(value_slot(5), 7, dev_y3)
    push(queries.at[0], queries.at[3], SEM_QUERY + 2, query_peers[2])

    for step in range(1, 4):
        arrived(queries.at[step], SEM_QUERY + step - 1, query_peers[step - 1])
        split_heads(step)
        attend(step - 1, 1)
        attend(step, 0)
        if step == 2:
            for i, (peer, other) in enumerate(head_peers):
                push(out_w_send.at[other], out_w_rows.at[h], SEM_W_OUT + i, peer)

    arrived(key_slot(5), SEM_KEY + 5, dev_y1)
    arrived(value_slot(6), SEM_VALUE + 6, dev_y3)
    arrived(key_slot(4), SEM_KEY + 4, dev_y3)
    arrived(value_slot(4), SEM_VALUE + 4, dev_y1)
    arrived(key_slot(7), SEM_KEY + 7, dev_y3)
    arrived(value_slot(7), SEM_VALUE + 7, dev_y1)

    for slot in range(4, 8):
        repeat_keys(columns(slot))
    for step in range(4, 8):
        attend(step - 1, 1)
        attend(step, 0)
    combine(0)
    heads_start(0)
    attend(7, 1)
    heads_on(0)
    combine(1)
    heads_start(1)
    heads_start(2)
    heads_end(0)
    heads_on(1)
    heads_on(2)

    for i, (peer, other) in enumerate(head_peers):
        arrived(out_w_rows.at[other], SEM_W_OUT + i, peer)

    def project(i):
        return jnp.dot(
            out_w_rows[i], heads[i].reshape(WIDTH, TOK), preferred_element_type=F32
        )

    attended[...] = project(h)
    for n, (some, upwards) in enumerate(PIECES):
        arrived(heads.at[h_chip, some], SEM_HEADS + 6 + n, dev_chip)
    attended[...] += project(h_chip)
    heads_end(1)
    heads_end(2)
    attended[...] += project(h_far)
    for n, (some, upwards) in enumerate(PIECES):
        arrived(heads.at[h_diag, some], SEM_HEADS + 9 + n, dev_chip)
    attended[...] += project(h_diag)
    store_attended = fetch(attended, attended_ref, 10)

    for c in started:
        c.wait_send()
    for slot in range(1, 4):
        for part_of in range(2):
            partial_copy(slot, part_of).wait_send()
    store_resnet.wait()
    store_attended.wait()


def on_device(
    feature, prev_feature, conv_weight, w_query, w_key, w_value, w_out, prev_keys, prev_values
):
    any_spec = pl.BlockSpec(memory_space=pl.ANY)
    vmem = pltpu.VMEM
    scratch = [
        vmem((4, TOK + 2 * COLS, WIDTH), BF16),
        vmem((TOK, WIDTH), BF16),
        vmem((2, 8, WIDTH), F32),
        vmem((7, 8, WIDTH), F32),
        vmem((3, 8, WIDTH), F32),
        vmem((4, 8, WIDTH), F32),
        vmem((WIDTH, WIDTH), F32),
        vmem((4, 8, WIDTH), F32),
        vmem((2, TOK + 2 * COLS, C // 2), BF16),
        vmem((9, WIDTH, C), BF16),
        vmem((3, WIDTH, C), BF16),
        vmem((3, TOK, WIDTH), F32),
        vmem((TOK, WIDTH), F32),
        vmem((4, TOK, WIDTH), BF16),
        vmem((TOK, C), BF16),
        vmem((4, HEADS_DEV, HEAD_DIM, TOK), BF16),
        vmem((4, HEADS_DEV, TOK, 2 * HEAD_DIM), BF16),
        vmem((HEADS_DEV, 2 * HEAD_DIM, 9 * TOK), BF16),
        vmem((HEADS_DEV, 2 * HEAD_DIM, 9 * TOK), BF16),
        vmem((3, 128, CHUNK), F32),
        vmem((3, 128, 128), F32),
        vmem((4, HEADS_DEV, 72, TOK), F32),
        vmem((3, HEADS_DEV, 80, TOK), BF16),
        vmem((3, HEADS_DEV, 80, TOK), BF16),
        vmem((2, TOK // 2, WIDTH), BF16),
        vmem((2, 2, COLS, WIDTH), BF16),
        vmem((HEADS_DEV, HEAD_DIM, TOK), BF16),
        vmem((4, HEADS_DEV, HEAD_DIM, TOK), BF16),
        vmem((WIDTH, C), BF16),
        vmem((4, WIDTH, WIDTH), BF16),
        vmem((4, WIDTH, WIDTH), BF16),
        vmem((WIDTH, TOK), F32),
        pltpu.SemaphoreType.DMA((SEMS,)),
        pltpu.SemaphoreType.DMA((SEMS,)),
        pltpu.SemaphoreType.DMA((11,)),
    ]
    resnet_out, attended = pl.pallas_call(
        kernel,
        out_shape=(
            jax.ShapeDtypeStruct((TOK, WIDTH), F32),
            jax.ShapeDtypeStruct((WIDTH, TOK), F32),
        ),
        in_specs=[any_spec] * 9,
        out_specs=(any_spec, any_spec),
        scratch_shapes=scratch,
        compiler_params=pltpu.CompilerParams(
            collective_id=0, has_side_effects=True, vmem_limit_bytes=60 * 2**20
        ),
    )(
        feature.reshape(TOK, WIDTH),
        prev_feature.reshape(TOK, WIDTH),
        conv_weight.reshape(9, C, WIDTH).transpose(0, 2, 1),
        w_query.T,
        w_key.T,
        w_value.T,
        w_out,
        prev_keys.T.reshape(HEADS_DEV, HEAD_DIM, TOK),
        prev_values.T.reshape(HEADS_DEV, HEAD_DIM, TOK),
    )
    return (resnet_out.reshape(feature.shape), attended.T)


def solution(mesh):
    placed = (
        P("patch", None, "head"),
        P("patch", None, "head"),
        P(None, None, None, "head"),
        P(None, "head"),
        P(None, "head"),
        P(None, "head"),
        P("head", None),
        P("patch", "head"),
        P("patch", "head"),
    )
    return jax.shard_map(
        on_device,
        mesh=mesh,
        in_specs=placed,
        out_specs=(P("patch", None, "head"), P("patch", "head")),
        check_vma=False,
    )
```

```python
import functools

import jax
import jax.numpy as jnp
from jax import lax
from jax.experimental import pallas as pl
from jax.experimental.pallas import tpu as pltpu
from jax.sharding import PartitionSpec as P

C = 1280
GROUPS = 32
HEAD_DIM = 64
TOK = 384
COLS = 96
WIDTH = 320
HEADS_DEV = 5
CHUNK = 4 * TOK
FIRST_OWN = 0
FIRST_OTHER = TOK
SECOND = 5 * TOK
PLACE = {0: 4, 1: 1, 2: 2, 3: 3, 4: 5, 5: 6, 6: 7, 7: 8}
NT = (((1,), (1,)), ((), ()))
N_PATCH = 32
COUNT = 128 * 96 * (C // GROUPS)
SCORE_SCALE = 1.4426950408889634 / HEAD_DIM**0.5
BF16 = jnp.bfloat16
F32 = jnp.float32
MESH = pl.DeviceIdType.MESH

SEM_FEATURE = 0
SEM_ROWS = 6
SEM_RIMS = 10
SEM_TOKENS = 12
SEM_W_OUT = 24
SEM_STATS_HEAD = 27
SEM_STATS_KEY = 30
SEM_STATS_QUERY = 37
SEM_QUERY = 40
SEM_KEY = 43
SEM_VALUE = 51
SEM_PARTIAL = 59
SEM_LEVEL = 74
SEM_HEADS = 89
SEMS = 109


def kernel(
    feature,
    prev_feature,
    conv_weight,
    w_query,
    w_key,
    w_value,
    w_out,
    prev_keys,
    prev_values,
    resnet_ref,
    attended_ref,
    raw,
    prev_in,
    sums_own,
    sums_key,
    sums_query,
    sums_head,
    groups,
    slopes,
    act,
    conv_w,
    qkv_w,
    conv_part,
    res_out,
    tokens,
    normed,
    queries,
    query_heads,
    key_t,
    value_t,
    scores,
    tops,
    part,
    partial_out,
    partial_in,
    level_out,
    level_in,
    relay_feature,
    relay_tokens,
    relay_heads,
    heads,
    out_w,
    out_w_send,
    out_w_rows,
    attended,
    send,
    recv,
    local,
):
    p = lax.axis_index("patch")
    h = lax.axis_index("head")
    x, y, zl = p // 8, (p // 2) % 4, p % 2

    def at(xx, yy, zz):
        return xx * 8 + yy * 2 + zz

    xn = x + 1 - 2 * (x % 2)
    xf = (x + 2) % 4
    y1, y2, y3 = (y + 1) % 4, (y + 2) % 4, (y + 3) % 4
    zh, core = h // 2, h % 2
    h_chip = zh * 2 + 1 - core
    h_far = (1 - zh) * 2 + core
    h_diag = (1 - zh) * 2 + 1 - core
    h_up = ((zh + zl) % 2) * 2 + core
    h_down = ((zh + 1 - zl) % 2) * 2 + core

    dev_chip, dev_far, dev_diag = (p, h_chip), (p, h_far), (p, h_diag)
    dev_up, dev_down = (at(x, y, 1 - zl), h_up), (at(x, y, 1 - zl), h_down)
    key_peers = [
        (at(x, y1, zl), h),
        (at(x, y3, zl), h),
        (at(x, y2, zl), h),
        (at(xf, y, zl), h),
        (at(xf, y1, zl), h),
        (at(xf, y3, zl), h),
        (at(xf, y2, zl), h),
    ]
    dev_y1, dev_y3, dev_y2, dev_xf = key_peers[:4]
    query_peers = [(at(x, y, 1 - zl), h), (at(xn, y, zl), h), (at(xn, y, 1 - zl), h)]
    p_next, p_prev = (p + 1) % N_PATCH, (p + N_PATCH - 1) % N_PATCH
    rim_peers = [(p_next, h), (p_next, h_far), (p_prev, h), (p_prev, h_far)]

    started = []

    def copy(src, dst, sem_send, sem_recv, device):
        return pltpu.make_async_remote_copy(
            src_ref=src,
            dst_ref=dst,
            send_sem=send.at[sem_send],
            recv_sem=recv.at[sem_recv],
            device_id=device,
            device_id_type=MESH,
        )

    def push(src, dst, sem, device, sem_send=None):
        c = copy(src, dst, sem if sem_send is None else sem_send, sem, device)
        c.start()
        started.append(c)

    def arrived(dst, sem, device):
        copy(dst, dst, sem, sem, device).wait_recv()

    def fetch(src, dst, sem):
        c = pltpu.make_async_copy(src, dst, local.at[sem])
        c.start()
        return c

    def columns(slot):
        return slice(PLACE[slot] * TOK, (PLACE[slot] + 1) * TOK)

    def key_slot(slot):
        return key_t.at[:, 0:HEAD_DIM, columns(slot)]

    def value_slot(slot):
        return value_t.at[:, 0:HEAD_DIM, columns(slot)]

    load_feature = fetch(feature, raw.at[h, 0:TOK], 0)
    load_prev = fetch(prev_feature, prev_in, 1)
    load_keys = fetch(prev_keys, key_slot(0), 2)
    load_values = fetch(prev_values, value_slot(0), 3)
    load_conv = fetch(conv_weight, conv_w, 4)
    load_q = fetch(w_query, qkv_w.at[0], 5)
    load_k = fetch(w_key, qkv_w.at[1], 6)
    load_v = fetch(w_value, qkv_w.at[2], 7)
    load_o = fetch(w_out, out_w, 8)

    barrier = pltpu.get_barrier_semaphore()
    peers = [dev_chip, dev_far, dev_diag, dev_up, dev_down]
    peers += key_peers + query_peers + rim_peers
    for peer in peers:
        pl.semaphore_signal(barrier, inc=1, device_id=peer, device_id_type=MESH)

    load_prev.wait()
    stale = prev_in[...].astype(F32)
    sums_own[0] = jnp.zeros((8, WIDTH), F32)
    sums_own[0, 0:1] = jnp.sum(stale, axis=0, keepdims=True)
    sums_own[0, 1:2] = jnp.sum(stale * stale, axis=0, keepdims=True)
    key_t[:, HEAD_DIM : 2 * HEAD_DIM, :] = jnp.zeros((HEADS_DEV, HEAD_DIM, 9 * TOK), BF16)
    query_heads[...] = jnp.zeros(query_heads.shape, BF16)
    value_t[:, HEAD_DIM : 2 * HEAD_DIM, :] = jnp.ones((HEADS_DEV, HEAD_DIM, 9 * TOK), BF16)
    load_o.wait()
    for i in range(4):
        out_w_send[i] = out_w[:, i * WIDTH : (i + 1) * WIDTH].T
    out_w_rows[h] = out_w_send[h]
    load_feature.wait()
    load_keys.wait()
    load_values.wait()

    row_group = (lax.broadcasted_iota(jnp.int32, (WIDTH, WIDTH), 0) * 1639) >> 16
    col_group = (lax.broadcasted_iota(jnp.int32, (WIDTH, WIDTH), 1) * 1639) >> 16
    same_group = jnp.where(row_group == col_group, 1.0, 0.0).astype(F32)
    groups[...] = same_group
    pl.semaphore_wait(barrier, len(peers))

    def relay_start(up, down, relay_up, relay_down, sem):
        push(up, relay_up, sem, dev_up)
        push(down, relay_down, sem + 1, dev_down)

    def relay_on(relay_up, relay_down, far_up, far_down, sem):
        arrived(relay_up, sem, dev_down)
        push(relay_up, far_up, sem + 2, dev_up)
        arrived(relay_down, sem + 1, dev_up)
        push(relay_down, far_down, sem + 3, dev_down)

    def relay_end(up, down, whole, sem):
        arrived(up, sem + 2, dev_down)
        arrived(down, sem + 3, dev_up)
        push(whole, whole, sem + 5, dev_chip)

    half = TOK // 2

    for i, peer in enumerate(key_peers):
        push(sums_own.at[0], sums_key.at[i], SEM_STATS_KEY + i, peer)

    relay_start(
        raw.at[h, 0:half],
        raw.at[h, half:TOK],
        relay_feature.at[0],
        relay_feature.at[1],
        SEM_FEATURE,
    )
    push(raw.at[h, 0:TOK], raw.at[h, 0:TOK], SEM_FEATURE + 4, dev_chip)
    above, below = slice(TOK, TOK + COLS), slice(TOK + COLS, TOK + 2 * COLS)
    for i in range(2):
        push(prev_in.at[TOK - COLS : TOK], raw.at[h, above], SEM_ROWS + i, rim_peers[i])
        push(prev_in.at[0:COLS], raw.at[h, below], SEM_ROWS + 2 + i, rim_peers[2 + i])

    total = sums_own[0]
    for i, peer in enumerate(key_peers):
        arrived(sums_key.at[i], SEM_STATS_KEY + i, peer)
        total = total + sums_key[i]
    sums_own[1] = total
    for i, peer in enumerate(query_peers):
        push(sums_own.at[1], sums_query.at[i], SEM_STATS_QUERY + i, peer)

    for i, peer in enumerate(query_peers):
        arrived(sums_query.at[i], SEM_STATS_QUERY + i, peer)
        total = total + sums_query[i]
    sums_head[h] = total
    head_peers = ((dev_chip, h_chip), (dev_far, h_far), (dev_diag, h_diag))
    for i, (peer, other) in enumerate(head_peers):
        push(sums_head.at[h], sums_head.at[h], SEM_STATS_HEAD + i, peer)

    def push_key(src, slot, device):
        push(src, key_slot(slot), SEM_KEY + slot, device)

    def push_value(src, slot, device):
        push(src, value_slot(slot), SEM_VALUE + slot, device)

    for slot, peer in ((3, dev_xf), (2, dev_y1), (1, dev_y3)):
        push_key(key_slot(0), slot, peer)
        push_value(value_slot(0), slot, peer)

    relay_on(
        relay_feature.at[0],
        relay_feature.at[1],
        raw.at[h_down, 0:half],
        raw.at[h_up, half:TOK],
        SEM_FEATURE,
    )
    for i, other in enumerate((h, h_far)):
        arrived(raw.at[other, above], SEM_ROWS + i, rim_peers[2 + i])
        arrived(raw.at[other, below], SEM_ROWS + 2 + i, rim_peers[i])
        rims = raw.at[other, TOK : TOK + 2 * COLS]
        push(rims, rims, SEM_RIMS + i, dev_chip)

    for i, (peer, other) in enumerate(head_peers):
        arrived(sums_head.at[other], SEM_STATS_HEAD + i, peer)
    group_sums = (
        jnp.dot(
            sums_head[...].reshape(32, WIDTH),
            groups[...],
            precision=lax.Precision.HIGHEST,
            preferred_element_type=F32,
        )
        * (1.0 / COUNT)
    )

    for i in range(4):
        centre = group_sums[8 * i : 8 * i + 1]
        square = group_sums[8 * i + 1 : 8 * i + 2]
        rstd = 0.5 * lax.rsqrt(square - centre * centre + 1e-05)
        slopes[i, 0:1] = rstd
        slopes[i, 1:2] = -centre * rstd

    def rims_of(other):
        return raw.at[other, TOK : TOK + 2 * COLS]

    arrived(rims_of(h_chip), SEM_RIMS, dev_chip)
    arrived(raw.at[h_chip, 0:TOK], SEM_FEATURE + 4, dev_chip)

    def activate(chip, place, src, dst, rows, inside):
        for c in range(2):
            i = chip * 2 + c
            v = raw[i, pl.ds(src, rows)].astype(F32) * slopes[i, 0:1] + slopes[i, 1:2]
            v = v + v * jnp.tanh(v)
            if inside is not None:
                v = jnp.where(inside, v, 0.0)
            act[place, pl.ds(dst, rows), c * WIDTH : (c + 1) * WIDTH] = v.astype(BF16)

    def activate_chip(chip, place):
        def body(t, carry):
            first = pl.multiple_of(t * 48, 48)
            activate(chip, place, first, pl.multiple_of(first + COLS, 48), 48, None)
            return carry

        lax.fori_loop(0, 8, body, 0)
        activate(chip, place, TOK, 0, COLS, p > 0)
        activate(chip, place, TOK + COLS, TOK + COLS, COLS, p < N_PATCH - 1)

    def convolve(place, chip, first, count):
        channels = pl.ds(pl.multiple_of(chip * (C // 2), 128), C // 2)

        def body(dx, carry):
            total = None
            for dy in range(3):
                product = lax.dot_general(
                    act[place, first + dy * COLS : first + dy * COLS + count],
                    conv_w[dy * 3 + dx, :, channels],
                    NT,
                    preferred_element_type=F32,
                )
                total = product if total is None else total + product
            if place == 0:
                conv_part[dx, first : first + count] = total
            else:
                conv_part[dx, first : first + count] += total
            return carry

        lax.fori_loop(0, 3, body, 0)

    activate_chip(zh, 0)
    load_conv.wait()
    relay_end(raw.at[h_far, 0:half], raw.at[h_far, half:TOK], raw.at[h_far, 0:TOK], SEM_FEATURE)
    convolve(0, zh, 0, TOK)
    arrived(rims_of(h_diag), SEM_RIMS + 1, dev_chip)
    arrived(raw.at[h_diag, 0:TOK], SEM_FEATURE + 5, dev_chip)
    activate_chip(1 - zh, 1)

    def conv_half(part_of):
        first = part_of * half
        convolve(1, 1 - zh, first, half)

        def merge_body(t, carry):
            rows = pl.ds(pl.multiple_of(t * COLS, COLS), COLS)
            col = lax.broadcasted_iota(jnp.int32, (COLS, WIDTH), 0)
            left = jnp.where(col == 0, 0.0, pltpu.roll(conv_part[0, rows], 1, axis=0))
            right = jnp.where(
                col == COLS - 1, 0.0, pltpu.roll(conv_part[2, rows], COLS - 1, axis=0)
            )
            result = raw[h, rows].astype(F32) + (conv_part[1, rows] + left + right)
            res_out[rows] = result
            tokens[h, rows] = result.astype(BF16)
            return carry

        lax.fori_loop(2 * part_of, 2 * part_of + 2, merge_body, 0)
        middle, last = first + COLS, first + half
        sem = SEM_TOKENS + 6 * part_of
        relay_start(
            tokens.at[h, first:middle],
            tokens.at[h, middle:last],
            relay_tokens.at[0, part_of],
            relay_tokens.at[1, part_of],
            sem,
        )
        push(tokens.at[h, first:last], tokens.at[h, first:last], sem + 4, dev_chip)

    def tokens_on(part_of):
        first, middle = part_of * half, part_of * half + COLS
        relay_on(
            relay_tokens.at[0, part_of],
            relay_tokens.at[1, part_of],
            tokens.at[h_down, first:middle],
            tokens.at[h_up, middle : first + half],
            SEM_TOKENS + 6 * part_of,
        )

    def tokens_end(part_of):
        first, middle, last = part_of * half, part_of * half + COLS, part_of * half + half
        relay_end(
            tokens.at[h_far, first:middle],
            tokens.at[h_far, middle:last],
            tokens.at[h_far, first:last],
            SEM_TOKENS + 6 * part_of,
        )

    def tokens_come(part_of):
        rows, sem = slice(part_of * half, part_of * half + half), SEM_TOKENS + 6 * part_of
        arrived(tokens.at[h_chip, rows], sem + 4, dev_chip)
        arrived(tokens.at[h_diag, rows], sem + 5, dev_chip)

    conv_half(0)
    arrived(key_slot(2), SEM_KEY + 2, dev_y3)
    push_key(key_slot(2), 4, dev_y1)
    arrived(value_slot(1), SEM_VALUE + 1, dev_y1)
    push_value(value_slot(1), 4, dev_y3)
    conv_half(1)
    store_resnet = fetch(res_out, resnet_ref, 9)
    tokens_on(0)
    arrived(key_slot(3), SEM_KEY + 3, dev_xf)
    push_key(key_slot(3), 6, dev_y1)
    push_key(key_slot(3), 5, dev_y3)
    arrived(value_slot(3), SEM_VALUE + 3, dev_xf)
    push_value(value_slot(3), 6, dev_y1)
    push_value(value_slot(3), 5, dev_y3)
    tokens_on(1)
    tokens_end(0)
    tokens_end(1)
    tokens_come(0)
    tokens_come(1)

    def norm_body(t, carry):
        rows = pl.ds(pl.multiple_of(t * COLS, COLS), COLS)
        parts = [tokens[i, rows].astype(F32) for i in range(4)]
        mean = sum(jnp.sum(v, axis=1, keepdims=True) for v in parts) * (1.0 / C)
        square = sum(jnp.sum(v * v, axis=1, keepdims=True) for v in parts) * (1.0 / C)
        rstd = lax.rsqrt(square - mean * mean + 1e-05)
        for i in range(4):
            normed[rows, i * WIDTH : (i + 1) * WIDTH] = ((parts[i] - mean) * rstd).astype(BF16)
        return carry

    lax.fori_loop(0, 4, norm_body, 0)

    def split_heads(slot):
        for i in range(HEADS_DEV):
            query_heads[slot, i, :, 0:HEAD_DIM] = queries[slot, i].T

    def project_tokens(i):
        result = lax.dot_general(qkv_w[i], normed[...], NT, preferred_element_type=F32)
        return result.astype(BF16).reshape(HEADS_DEV, HEAD_DIM, TOK)

    load_q.wait()
    queries[0] = project_tokens(0)
    for i, peer in enumerate(query_peers[:2]):
        push(queries.at[0], queries.at[i + 1], SEM_QUERY + i, peer)
    load_k.wait()
    key_t[:, 0:HEAD_DIM, 0:TOK] = project_tokens(1)
    load_v.wait()
    value_t[:, 0:HEAD_DIM, 0:TOK] = project_tokens(2)
    split_heads(0)

    lane = lax.broadcasted_iota(jnp.int32, (128, 128), 1)

    def score_rows(slot, first, i, t):
        rows = slice(t * 128, (t + 1) * 128)
        result = jnp.dot(
            query_heads[slot, i, rows],
            key_t[i, :, first : first + CHUNK],
            preferred_element_type=F32,
        )
        scores[t] = result
        tops[t] = functools.reduce(
            jnp.maximum, [result[:, 128 * k : 128 * (k + 1)] for k in range(CHUNK // 128)]
        )

    def weigh_rows(slot, first, i, t):
        rows = slice(t * 128, (t + 1) * 128)
        top = jnp.max(tops[t], axis=1, keepdims=True) * SCORE_SCALE
        weights = jnp.exp2(scores[t] * SCORE_SCALE - top).astype(BF16)
        summed = lax.dot_general(
            weights, value_t[i, :, first : first + CHUNK], NT, preferred_element_type=F32
        )
        turned = jnp.where(lane == 65, top, summed).T
        if first != SECOND:
            part[slot, i, :, rows] = turned[0:72]
            return
        before = part[slot, i, :, rows]
        level = jnp.maximum(before[65:66], turned[65:66])
        both = before[0:65] * jnp.exp2(before[65:66] - level) + turned[0:65] * jnp.exp2(
            turned[65:66] - level
        )
        result = both[0:64] / both[64:65]
        lse = level + jnp.log2(both[64:65])
        if slot == 0:
            part[0, i, 0:64, rows] = result
        else:
            partial_out[slot - 1, i, :, rows] = result.astype(BF16)
        level_out[slot, i, :, rows] = jnp.broadcast_to(lse, (8, 128))

    def partial_copies(slot, i):
        n = (slot - 1) * HEADS_DEV + i
        return (
            copy(
                partial_out.at[slot - 1, i],
                partial_in.at[slot - 1, i],
                SEM_PARTIAL + n,
                SEM_PARTIAL + n,
                query_peers[slot - 1],
            ),
            copy(
                level_out.at[slot, i],
                level_in.at[slot - 1, i],
                SEM_LEVEL + n,
                SEM_LEVEL + n,
                query_peers[slot - 1],
            ),
        )

    def send_partial(slot, first, i):
        if slot > 0 and first == SECOND:
            for c in partial_copies(slot, i):
                c.start()

    steps = [(0, FIRST_OWN)]
    steps += [(slot, FIRST_OTHER) for slot in (1, 2, 3)]
    steps += [(slot, SECOND) for slot in (3, 2, 1, 0)]

    def attend(step):
        slot, first = steps[step]

        def body(pair, carry):
            for i in (2 * pair, 2 * pair + 1):
                score_rows(slot, first, i, 1)
                weigh_rows(slot, first, i, 0)
                score_rows(slot, first, i, 2)
                weigh_rows(slot, first, i, 1)
                score_rows(slot, first, i + 1, 0)
                weigh_rows(slot, first, i, 2)
            for i in (2 * pair, 2 * pair + 1):
                send_partial(slot, first, i)
            return carry

        lax.fori_loop(0, (HEADS_DEV - 1) // 2, body, 0)

    def attend_head(slot, first, i, following):
        def body(unused, carry):
            score_rows(slot, first, i, 1)
            weigh_rows(slot, first, i, 0)
            score_rows(slot, first, i, 2)
            weigh_rows(slot, first, i, 1)
            if following is not None:
                score_rows(*following, 0)
            weigh_rows(slot, first, i, 2)
            send_partial(slot, first, i)
            return carry

        lax.fori_loop(0, 1, body, 0)

    def attend_last(step):
        attend_head(*steps[step], HEADS_DEV - 1, (*steps[step + 1], 0))

    def combine(i):
        for r in range(3):
            for c in partial_copies(r + 1, i):
                c.wait_recv()
        levels = [level_out[0, i, 0:1]] + [level_in[r, i, 0:1] for r in range(3)]
        top = functools.reduce(jnp.maximum, levels)
        shares = [jnp.exp2(level - top) for level in levels]
        whole = 1.0 / sum(shares)
        result = part[0, i, 0:64] * (shares[0] * whole)
        for r in range(3):
            result = result + partial_in[r, i].astype(F32) * (shares[r + 1] * whole)
        heads[h, i] = result.astype(BF16)
        push(heads.at[h, i], relay_heads.at[i], SEM_HEADS + i, dev_down if i % 2 else dev_up)
        push(heads.at[h, i], heads.at[h, i], SEM_HEADS + 10 + i, dev_chip)

    def heads_on(i):
        source, target = (dev_up, dev_down) if i % 2 else (dev_down, dev_up)
        arrived(relay_heads.at[i], SEM_HEADS + i, source)
        far = heads.at[h_up if i % 2 else h_down, i]
        push(relay_heads.at[i], far, SEM_HEADS + 5 + i, target)

    def heads_end(i):
        far = heads.at[h_far, i]
        arrived(far, SEM_HEADS + 5 + i, dev_up if i % 2 else dev_down)
        push(far, far, SEM_HEADS + 15 + i, dev_chip)

    arrived(key_slot(1), SEM_KEY + 1, dev_y1)
    arrived(value_slot(2), SEM_VALUE + 2, dev_y3)
    score_rows(0, FIRST_OWN, 0, 0)
    attend(0)
    arrived(key_slot(6), SEM_KEY + 6, dev_y3)
    push_key(key_slot(6), 7, dev_y1)
    arrived(value_slot(5), SEM_VALUE + 5, dev_y1)
    push_value(value_slot(5), 7, dev_y3)
    push(queries.at[0], queries.at[3], SEM_QUERY + 2, query_peers[2])

    for step in range(1, 4):
        arrived(queries.at[step], SEM_QUERY + step - 1, query_peers[step - 1])
        split_heads(step)
        attend_last(step - 1)
        attend(step)
        if step == 2:
            for i, (peer, other) in enumerate(head_peers):
                push(out_w_send.at[other], out_w_rows.at[h], SEM_W_OUT + i, peer)

    arrived(key_slot(5), SEM_KEY + 5, dev_y1)
    arrived(value_slot(6), SEM_VALUE + 6, dev_y3)
    arrived(key_slot(4), SEM_KEY + 4, dev_y3)
    arrived(value_slot(4), SEM_VALUE + 4, dev_y1)
    arrived(key_slot(7), SEM_KEY + 7, dev_y3)
    arrived(value_slot(7), SEM_VALUE + 7, dev_y1)

    for step in range(4, 7):
        attend_last(step - 1)
        attend(step)
    attend_last(6)
    for i in range(HEADS_DEV):
        attend_head(0, SECOND, i, (0, SECOND, i + 1) if i + 1 < HEADS_DEV else None)
        combine(i)
        if i > 0:
            heads_on(i - 1)
        if i > 1:
            heads_end(i - 2)
    heads_on(HEADS_DEV - 1)
    heads_end(HEADS_DEV - 2)

    for i, (peer, other) in enumerate(head_peers):
        arrived(out_w_rows.at[other], SEM_W_OUT + i, peer)

    def project(i):
        return jnp.dot(
            out_w_rows[i], heads[i].reshape(WIDTH, TOK), preferred_element_type=F32
        )

    attended[...] = project(h)
    for i in range(HEADS_DEV):
        arrived(heads.at[h_chip, i], SEM_HEADS + 10 + i, dev_chip)
    attended[...] += project(h_chip)
    heads_end(HEADS_DEV - 1)
    attended[...] += project(h_far)
    for i in range(HEADS_DEV):
        arrived(heads.at[h_diag, i], SEM_HEADS + 15 + i, dev_chip)
    attended[...] += project(h_diag)
    store_attended = fetch(attended, attended_ref, 10)

    for c in started:
        c.wait_send()
    for slot in range(1, 4):
        for i in range(HEADS_DEV):
            for c in partial_copies(slot, i):
                c.wait_send()
    store_resnet.wait()
    store_attended.wait()


def on_device(
    feature, prev_feature, conv_weight, w_query, w_key, w_value, w_out, prev_keys, prev_values
):
    any_spec = pl.BlockSpec(memory_space=pl.ANY)
    vmem = pltpu.VMEM
    scratch = [
        vmem((4, TOK + 2 * COLS, WIDTH), BF16),
        vmem((TOK, WIDTH), BF16),
        vmem((2, 8, WIDTH), F32),
        vmem((7, 8, WIDTH), F32),
        vmem((3, 8, WIDTH), F32),
        vmem((4, 8, WIDTH), F32),
        vmem((WIDTH, WIDTH), F32),
        vmem((4, 8, WIDTH), F32),
        vmem((2, TOK + 2 * COLS, C // 2), BF16),
        vmem((9, WIDTH, C), BF16),
        vmem((3, WIDTH, C), BF16),
        vmem((3, TOK, WIDTH), F32),
        vmem((TOK, WIDTH), F32),
        vmem((4, TOK, WIDTH), BF16),
        vmem((TOK, C), BF16),
        vmem((4, HEADS_DEV, HEAD_DIM, TOK), BF16),
        vmem((4, HEADS_DEV, TOK, 2 * HEAD_DIM), BF16),
        vmem((HEADS_DEV, 2 * HEAD_DIM, 9 * TOK), BF16),
        vmem((HEADS_DEV, 2 * HEAD_DIM, 9 * TOK), BF16),
        vmem((3, 128, CHUNK), F32),
        vmem((3, 128, 128), F32),
        vmem((4, HEADS_DEV, 72, TOK), F32),
        vmem((3, HEADS_DEV, HEAD_DIM, TOK), BF16),
        vmem((3, HEADS_DEV, HEAD_DIM, TOK), BF16),
        vmem((4, HEADS_DEV, 8, TOK), F32),
        vmem((3, HEADS_DEV, 8, TOK), F32),
        vmem((2, TOK // 2, WIDTH), BF16),
        vmem((2, 2, COLS, WIDTH), BF16),
        vmem((HEADS_DEV, HEAD_DIM, TOK), BF16),
        vmem((4, HEADS_DEV, HEAD_DIM, TOK), BF16),
        vmem((WIDTH, C), BF16),
        vmem((4, WIDTH, WIDTH), BF16),
        vmem((4, WIDTH, WIDTH), BF16),
        vmem((WIDTH, TOK), F32),
        pltpu.SemaphoreType.DMA((SEMS,)),
        pltpu.SemaphoreType.DMA((SEMS,)),
        pltpu.SemaphoreType.DMA((11,)),
    ]
    resnet_out, attended = pl.pallas_call(
        kernel,
        out_shape=(
            jax.ShapeDtypeStruct((TOK, WIDTH), F32),
            jax.ShapeDtypeStruct((WIDTH, TOK), F32),
        ),
        in_specs=[any_spec] * 9,
        out_specs=(any_spec, any_spec),
        scratch_shapes=scratch,
        compiler_params=pltpu.CompilerParams(
            collective_id=0, has_side_effects=True, vmem_limit_bytes=60 * 2**20
        ),
    )(
        feature.reshape(TOK, WIDTH),
        prev_feature.reshape(TOK, WIDTH),
        conv_weight.reshape(9, C, WIDTH).transpose(0, 2, 1),
        w_query.T,
        w_key.T,
        w_value.T,
        w_out,
        prev_keys.T.reshape(HEADS_DEV, HEAD_DIM, TOK),
        prev_values.T.reshape(HEADS_DEV, HEAD_DIM, TOK),
    )
    return (resnet_out.reshape(feature.shape), attended.T)


def solution(mesh):
    placed = (
        P("patch", None, "head"),
        P("patch", None, "head"),
        P(None, None, None, "head"),
        P(None, "head"),
        P(None, "head"),
        P(None, "head"),
        P("head", None),
        P("patch", "head"),
        P("patch", "head"),
    )
    return jax.shard_map(
        on_device,
        mesh=mesh,
        in_specs=placed,
        out_specs=(P("patch", None, "head"), P("patch", "head")),
        check_vma=False,
    )
```
